32 devices in a mesh: dp: 8 (over y, x, core), block: 4 (over z).
Axes of the slice: x: 2, y: 2, z: 4, core: 2. Of those that a mesh axis runs over, the one named last changes fastest.
Arguments:
- tokens: bfloat16 [2304, 6144], P('dp', 'block'), may hold values from -6 to 6
- up_first: bfloat16 [96, 64, 256], P('block'), may hold values from -0.75 to 0.75
- up_mix: bfloat16 [256, 96, 96], replicated, may hold values from -0.625 to 0.625
- down_mix: bfloat16 [256, 96, 96], replicated, may hold values from -0.625 to 0.625
- down_last: bfloat16 [96, 64, 256], P('block'), may hold values from -0.375 to 0.375
- cotangent: bfloat16 [2304, 6144], P('dp', 'block'), may hold values from -6 to 6
Outputs:
- encoded: bfloat16 [2304, 6144], P('dp', 'block')
- grad_tokens: bfloat16 [2304, 6144], P('dp', 'block')
- grad_up_first: float32 [96, 64, 256], P('block')
- grad_down_last: float32 [96, 64, 256], P('block')
The draws below stay inside these ranges and needn't reach their ends.
All inputs are finite; a program needn't handle non-finite values.
Results may differ from the reference program's by a relative error of at most 0.014.
Values may be sent and summed in bfloat16 or wider, within the bound.
A program may use at most 128 MiB of HBM per device.

```python
import jax
import jax.numpy as jnp
from jax import lax

D = 6144
NB = 96
BIN = 64
BH = 256
TOK_DEV = 288
TOKENS = 2304
N_DP = 8


def block_levels(own_key, extent, cuts, smallest, largest):
    factor_of, own = 1.0, jax.random.fold_in(own_key, 6)
    for dim, blocks in cuts:
        steps = jnp.exp(jax.random.uniform(jax.random.fold_in(own, dim), (blocks,), jnp.float32, smallest / len(cuts), largest / len(cuts)))
        factor_of = factor_of * jnp.repeat(steps, extent[dim] // blocks).reshape([-1 if axis == dim else 1 for axis in range(len(extent))])
    return factor_of


def normal_values(key, dims, spread, limit, split=(), kind=jnp.bfloat16):
    values = spread * jax.random.normal(key, dims, jnp.float32)
    if split:
        values = values * block_levels(key, dims, split, -0.22, 0.18)
    return jnp.clip(values, -limit, limit).astype(kind)


def setup_inputs(seed: int = 0) -> dict:
    seeds = jax.random.split(jax.random.key(seed), 7)
    tokens = normal_values(seeds[0], (TOKENS, D), 1.0, 6.0, ((0, 8), (1, 4)))
    up_first = normal_values(seeds[1], (NB, BIN, BH), BIN ** -0.5, 0.75, ((0, 4),))
    up_mix = normal_values(seeds[2], (BH, NB, NB), NB ** -0.5, 0.625)
    down_mix = normal_values(seeds[3], (BH, NB, NB), NB ** -0.5, 0.625)
    down_last = normal_values(seeds[4], (NB, BIN, BH), BH ** -0.5, 0.375, ((0, 4),))
    cotangent = normal_values(seeds[5], (TOKENS, D), 1.0, 6.0, ((0, 8), (1, 4)))
    return dict(tokens=tokens, up_first=up_first, up_mix=up_mix, down_mix=down_mix, down_last=down_last, cotangent=cotangent)


gelu_coef = 0.7978845608028654
cubic_coef = 0.044715


def gelu_pair(values):
    inner = gelu_coef * (values + cubic_coef * values * values * values)
    tangent = jnp.tanh(inner)
    result = 0.5 * values * (1.0 + tangent)
    slope = 0.5 * (1.0 + tangent) + 0.5 * values * (1.0 - tangent * tangent) * gelu_coef * (1.0 + 3.0 * cubic_coef * values * values)
    return result, slope


def reference(tokens, up_first, up_mix, down_mix, down_last, cotangent):
    flt = jnp.float32
    half = jnp.bfloat16
    inputs = tokens.reshape(N_DP, TOK_DEV, NB, BIN)
    outgrads = cotangent.reshape(N_DP, TOK_DEV, NB, BIN)
    first_w = up_first.astype(flt)
    upmix_w = up_mix.astype(flt)
    downmix_w = down_mix.astype(flt)
    last_w = down_last.astype(flt)

    def one_block(totals, pieces):
        inblock, gblock = pieces
        inblock = inblock.astype(flt)
        gblock = gblock.astype(flt)
        first = jnp.einsum('trk,rkc->trc', inblock, first_w).astype(half)
        preact = jnp.einsum('trc,csr->tsc', first.astype(flt), upmix_w).astype(half)
        hidden_f, slope = gelu_pair(preact.astype(flt))
        hidden = hidden_f.astype(half)
        mixed = jnp.einsum('tsc,cqs->tqc', hidden.astype(flt), downmix_w).astype(half)
        encoded = jnp.einsum('tqc,qkc->tqk', mixed.astype(flt), last_w).astype(half)
        grad_mixed = jnp.einsum('tqk,qkc->tqc', gblock, last_w).astype(half)
        grad_last = jnp.einsum('tqk,tqc->qkc', gblock, mixed.astype(flt))
        grad_hidden = jnp.einsum('tqc,cqs->tsc', grad_mixed.astype(flt), downmix_w).astype(half)
        grad_pre = (grad_hidden.astype(flt) * slope).astype(half)
        grad_first = jnp.einsum('tsc,csr->trc', grad_pre.astype(flt), upmix_w).astype(half)
        grad_in = jnp.einsum('trc,rkc->trk', grad_first.astype(flt), first_w).astype(half)
        grad_firstw = jnp.einsum('trk,trc->rkc', inblock, grad_first.astype(flt))
        return (totals[0] + grad_firstw, totals[1] + grad_last), (encoded, grad_in)

    zeros = (jnp.zeros((NB, BIN, BH), flt), jnp.zeros((NB, BIN, BH), flt))
    totals, outputs = lax.scan(one_block, zeros, (inputs, outgrads))
    encoded = outputs[0].reshape(TOKENS, D)
    grad_tokens = outputs[1].reshape(TOKENS, D)
    return (encoded, grad_tokens, totals[0], totals[1])
```

```python
import jax
import jax.numpy as jnp
from jax import lax
from jax.sharding import PartitionSpec as P

gelu_coef = 0.7978845608028654
cubic_coef = 0.044715
WIRE = jnp.bfloat16


def gelu_pair(values):
    inner = gelu_coef * (values + cubic_coef * values * values * values)
    tangent = jnp.tanh(inner)
    result = 0.5 * values * (1.0 + tangent)
    slope = 0.5 * (1.0 + tangent) + 0.5 * values * (1.0 - tangent * tangent) * gelu_coef * (
        1.0 + 3.0 * cubic_coef * values * values
    )
    return (result, slope)


def gather_weights(weights, n_dp, n_block):
    two, blocks, width, hidden = weights.shape
    part = width // n_dp
    mine = lax.dynamic_slice_in_dim(weights, lax.axis_index("dp") * part, part, 2)
    full = lax.all_gather(mine, ("block", "dp"))
    full = full.reshape(n_block, n_dp, two, blocks, part, hidden)
    full = full.transpose(2, 0, 3, 1, 4, 5)
    return full.reshape(two, n_block * blocks, width, hidden)


def scatter_grad(grad, n_dp, n_block):
    blocks, width, hidden = grad.shape
    local = blocks // n_block
    part = width // n_dp
    pieces = grad.astype(WIRE).reshape(n_block, local, n_dp, part, hidden).transpose(0, 2, 1, 3, 4)
    pieces = pieces.reshape(n_block * n_dp, local, part, hidden)
    return lax.psum_scatter(pieces, ("block", "dp"), scatter_dimension=0, tiled=True)


def spread_grads(first, last):
    full = lax.all_gather(jnp.concatenate([first, last], 0), "dp")
    n_dp, two, blocks, part, hidden = full.shape
    full = full.transpose(1, 2, 0, 3, 4).reshape(two, blocks, n_dp * part, hidden)
    full = full.astype(jnp.float32)
    return full[0], full[1]


def shards(tokens, up_first, up_mix, down_mix, down_last, cotangent, n_dp, n_block):
    flt = jnp.float32
    half = jnp.bfloat16
    rows, features = tokens.shape
    width = up_first.shape[1]
    mine = rows // n_block
    blocks = up_first.shape[0] * n_block
    both = jnp.stack([tokens.reshape(n_block, mine, features), cotangent.reshape(n_block, mine, features)], 1)
    both = lax.all_to_all(both, "block", 0, 0, tiled=True)
    both = both.reshape(n_block, 2, mine, up_first.shape[0], width)
    both = both.transpose(1, 0, 3, 2, 4).reshape(2, blocks, mine, width)
    inputs, outgrads = both[0], both[1]
    weights = gather_weights(jnp.stack([up_first, down_last]), n_dp, n_block)
    first_w, last_w = weights[0], weights[1]
    first = jnp.einsum("rtk,rkc->rtc", inputs, first_w, preferred_element_type=flt).astype(half)
    grad_mixed = jnp.einsum("qtk,qkc->qtc", outgrads, last_w, preferred_element_type=flt).astype(half)
    pre = jnp.einsum("rtc,csr->tsc", first, up_mix, preferred_element_type=flt).astype(half)
    hidden_f, slope = gelu_pair(pre.astype(flt))
    hidden = hidden_f.astype(half)
    mixed = jnp.einsum("tsc,cqs->qtc", hidden, down_mix, preferred_element_type=flt).astype(half)
    grad_last = jnp.einsum("qtk,qtc->qkc", outgrads, mixed, preferred_element_type=flt)
    part_last = scatter_grad(grad_last, n_dp, n_block)
    encoded = jnp.einsum("qtc,qkc->qtk", mixed, last_w, preferred_element_type=flt).astype(half)
    grad_hidden = jnp.einsum("qtc,cqs->tsc", grad_mixed, down_mix, preferred_element_type=flt).astype(half)
    grad_pre = (grad_hidden.astype(flt) * slope).astype(half)
    grad_first = jnp.einsum("tsc,csr->rtc", grad_pre, up_mix, preferred_element_type=flt).astype(half)
    grad_firstw = jnp.einsum("rtk,rtc->rkc", inputs, grad_first, preferred_element_type=flt)
    part_first = scatter_grad(grad_firstw, n_dp, n_block)
    grad_in = jnp.einsum("rtc,rkc->rtk", grad_first, first_w, preferred_element_type=flt).astype(half)
    outs = jnp.stack([encoded, grad_in]).reshape(2, n_block, blocks // n_block, mine, width)
    outs = outs.transpose(1, 0, 3, 2, 4).reshape(n_block, 2, mine, features)
    outs = lax.all_to_all(outs, "block", 0, 0, tiled=True)
    summed_first, summed_last = spread_grads(part_first, part_last)
    return (
        outs[:, 0].reshape(rows, features),
        outs[:, 1].reshape(rows, features),
        summed_first,
        summed_last,
    )


def solution(mesh):
    n_dp, n_block = mesh.shape["dp"], mesh.shape["block"]

    def run(*args):
        return shards(*args, n_dp, n_block)

    placed = (
        P("dp", "block"),
        P("block", None, None),
        P(),
        P(),
        P("block", None, None),
        P("dp", "block"),
    )
    return jax.shard_map(
        run,
        mesh=mesh,
        in_specs=placed,
        out_specs=(
            P("dp", "block"),
            P("dp", "block"),
            P("block", None, None),
            P("block", None, None),
        ),
        check_vma=False,
    )
```

```python
import jax
import jax.numpy as jnp
from jax import lax
from jax.sharding import PartitionSpec as P

gelu_coef = 0.7978845608028654
cubic_coef = 0.044715


def gelu_pair(values):
    inner = gelu_coef * (values + cubic_coef * values * values * values)
    tangent = jnp.tanh(inner)
    result = 0.5 * values * (1.0 + tangent)
    slope = 0.5 * (1.0 + tangent) + 0.5 * values * (1.0 - tangent * tangent) * gelu_coef * (
        1.0 + 3.0 * cubic_coef * values * values
    )
    return (result, slope)


def gather_weights(weights, n_dp, n_block):
    two, blocks, width, hidden = weights.shape
    part = width // n_dp
    mine = lax.dynamic_slice_in_dim(weights, lax.axis_index("dp") * part, part, 2)
    full = lax.all_gather(mine, ("block", "dp"))
    full = full.reshape(n_block, n_dp, two, blocks, part, hidden)
    full = full.transpose(2, 0, 3, 1, 4, 5)
    return full.reshape(two, n_block * blocks, width, hidden)


def to_blocks(panel):
    return lax.all_to_all(panel, "block", split_axis=1, concat_axis=0, tiled=True)


def shards(tokens, up_first, up_mix, down_mix, down_last, cotangent, n_dp, n_block):
    flt = jnp.float32
    half = jnp.bfloat16
    rows, features = tokens.shape
    width = up_first.shape[1]
    mine = rows // n_block
    blocks = up_first.shape[0] * n_block
    both = jnp.stack([tokens.reshape(n_block, mine, features), cotangent.reshape(n_block, mine, features)], 1)
    both = lax.all_to_all(both, "block", 0, 0, tiled=True)
    both = both.reshape(n_block, 2, mine, up_first.shape[0], width)
    both = both.transpose(1, 0, 3, 2, 4).reshape(2, blocks, mine, width)
    inputs, outgrads = both[0], both[1]
    weights = gather_weights(jnp.stack([up_first, down_last]), n_dp, n_block)
    first_w, last_w = weights[0], weights[1]
    first = jnp.einsum("rtk,rkc->rtc", inputs, first_w, preferred_element_type=flt).astype(half)
    grad_mixed = jnp.einsum("qtk,qkc->qtc", outgrads, last_w, preferred_element_type=flt).astype(half)
    pre = jnp.einsum("rtc,csr->tsc", first, up_mix, preferred_element_type=flt).astype(half)
    hidden_f, slope = gelu_pair(pre.astype(flt))
    hidden = hidden_f.astype(half)
    mixed_tok = jnp.einsum("tsc,cqs->tqc", hidden, down_mix, preferred_element_type=flt).astype(half)
    mixed = to_blocks(mixed_tok)
    grad_hidden = jnp.einsum("qtc,cqs->tsc", grad_mixed, down_mix, preferred_element_type=flt).astype(half)
    grad_pre = (grad_hidden.astype(flt) * slope).astype(half)
    grad_first_tok = jnp.einsum("tsc,csr->trc", grad_pre, up_mix, preferred_element_type=flt).astype(half)
    own_in = tokens.reshape(rows, up_first.shape[0], width)
    own_out = cotangent.reshape(rows, up_first.shape[0], width)
    grad_last = jnp.einsum("tqk,tqc->qkc", own_out, mixed, preferred_element_type=flt)
    summed_last = lax.psum(grad_last, "dp")
    grad_first = to_blocks(grad_first_tok)
    encoded = jnp.einsum("tqc,qkc->tqk", mixed, down_last, preferred_element_type=flt).astype(half)
    grad_firstw = jnp.einsum("trk,trc->rkc", own_in, grad_first, preferred_element_type=flt)
    summed_first = lax.psum(grad_firstw, "dp")
    grad_in = jnp.einsum("trc,rkc->trk", grad_first, up_first, preferred_element_type=flt).astype(half)
    return (
        encoded.reshape(rows, features),
        grad_in.reshape(rows, features),
        summed_first,
        summed_last,
    )


def solution(mesh):
    n_dp, n_block = mesh.shape["dp"], mesh.shape["block"]

    def run(*args):
        return shards(*args, n_dp, n_block)

    placed = (
        P("dp", "block"),
        P("block", None, None),
        P(),
        P(),
        P("block", None, None),
        P("dp", "block"),
    )
    return jax.shard_map(
        run,
        mesh=mesh,
        in_specs=placed,
        out_specs=(
            P("dp", "block"),
            P("dp", "block"),
            P("block", None, None),
            P("block", None, None),
        ),
        check_vma=False,
    )
```

```python
import jax
import jax.numpy as jnp
from jax import lax
from jax.sharding import PartitionSpec as P

gelu_coef = 0.7978845608028654
cubic_coef = 0.044715


def gelu_pair(values):
    inner = gelu_coef * (values + cubic_coef * values * values * values)
    tangent = jnp.tanh(inner)
    result = 0.5 * values * (1.0 + tangent)
    slope = 0.5 * (1.0 + tangent) + 0.5 * values * (1.0 - tangent * tangent) * gelu_coef * (
        1.0 + 3.0 * cubic_coef * values * values
    )
    return (result, slope)


def gather_weights(weights, n_dp, n_block):
    two, blocks, width, hidden = weights.shape
    part = width // n_dp
    mine = lax.dynamic_slice_in_dim(weights, lax.axis_index("dp") * part, part, 2)
    full = lax.all_gather(mine, ("block", "dp"))
    full = full.reshape(n_block, n_dp, two, blocks, part, hidden)
    full = full.transpose(2, 0, 3, 1, 4, 5)
    return full.reshape(two, n_block * blocks, width, hidden)


def to_blocks(panel):
    return lax.all_to_all(panel, "block", split_axis=1, concat_axis=0, tiled=True)


def shards(tokens, up_first, up_mix, down_mix, down_last, cotangent, n_dp, n_block):
    flt = jnp.float32
    half = jnp.bfloat16
    rows, features = tokens.shape
    width = up_first.shape[1]
    mine = rows // n_block
    blocks = up_first.shape[0] * n_block
    both = jnp.stack([tokens.reshape(n_block, mine, features), cotangent.reshape(n_block, mine, features)], 1)
    both = lax.all_to_all(both, "block", 0, 0, tiled=True)
    both = both.reshape(n_block, 2, mine, up_first.shape[0], width)
    both = both.transpose(1, 0, 3, 2, 4).reshape(2, blocks, mine, width)
    inputs, outgrads = both[0], both[1]
    first_w = gather_weights(up_first[None], n_dp, n_block)[0]
    later, first_w = lax.optimization_barrier((down_last, first_w))
    last_w = gather_weights(later[None], n_dp, n_block)[0]
    first = jnp.einsum("rtk,rkc->rtc", inputs, first_w, preferred_element_type=flt).astype(half)
    grad_mixed = jnp.einsum("qtk,qkc->qtc", outgrads, last_w, preferred_element_type=flt).astype(half)
    pre = jnp.einsum("rtc,csr->tsc", first, up_mix, preferred_element_type=flt).astype(half)
    hidden_f, slope = gelu_pair(pre.astype(flt))
    hidden = hidden_f.astype(half)
    mixed_tok = jnp.einsum("tsc,cqs->tqc", hidden, down_mix, preferred_element_type=flt).astype(half)
    mixed = to_blocks(mixed_tok)
    grad_hidden = jnp.einsum("qtc,cqs->tsc", grad_mixed, down_mix, preferred_element_type=flt).astype(half)
    grad_pre = (grad_hidden.astype(flt) * slope).astype(half)
    grad_first_tok = jnp.einsum("tsc,csr->trc", grad_pre, up_mix, preferred_element_type=flt).astype(half)
    own_in = tokens.reshape(rows, up_first.shape[0], width)
    own_out = cotangent.reshape(rows, up_first.shape[0], width)
    grad_last = jnp.einsum("tqk,tqc->qkc", own_out, mixed, preferred_element_type=flt)
    summed_last = lax.psum(grad_last, "dp")
    grad_first = to_blocks(grad_first_tok)
    encoded = jnp.einsum("tqc,qkc->tqk", mixed, down_last, preferred_element_type=flt).astype(half)
    grad_firstw = jnp.einsum("trk,trc->rkc", own_in, grad_first, preferred_element_type=flt)
    grad_firstw, summed_last = lax.optimization_barrier((grad_firstw, summed_last))
    summed_first = lax.psum(grad_firstw, "dp")
    grad_in = jnp.einsum("trc,rkc->trk", grad_first, up_first, preferred_element_type=flt).astype(half)
    return (
        encoded.reshape(rows, features),
        grad_in.reshape(rows, features),
        summed_first,
        summed_last,
    )


def solution(mesh):
    n_dp, n_block = mesh.shape["dp"], mesh.shape["block"]

    def run(*args):
        return shards(*args, n_dp, n_block)

    placed = (
        P("dp", "block"),
        P("block", None, None),
        P(),
        P(),
        P("block", None, None),
        P("dp", "block"),
    )
    return jax.shard_map(
        run,
        mesh=mesh,
        in_specs=placed,
        out_specs=(
            P("dp", "block"),
            P("dp", "block"),
            P("block", None, None),
            P("block", None, None),
        ),
        check_vma=False,
    )
```
